32 devices in a mesh: section: 2 (over x), dp: 16 (over z, y, core).
Axes of the slice: x: 2, y: 2, z: 4, core: 2. Of those that a mesh axis runs over, the one named last changes fastest.
Arguments:
- enc_in: bfloat16 [64, 16, 16, 320], P(('dp', 'section')), parts along dimension 0, may hold values from -6 to 6
- dec_in: bfloat16 [64, 16, 16, 320], P(('dp', 'section')), parts along dimension 0, may hold values from -6 to 6
- fresh: bfloat16 [32, 16, 16, 320], P('dp'), parts along dimension 0, may hold values from -6 to 6
- skip_queue: bfloat16 [128, 16, 16, 320], P(('dp', 'section')), parts along dimension 0, may hold values from -6 to 6
- enc_weight: bfloat16 [2, 3, 3, 320, 320], P('section'), may hold values from -0.109375 to 0.109375
- enc_bias: float32 [2, 320], P('section'), may hold values from -2 to 2
- enc_gain: float32 [2, 320], P('section'), may hold values from 0.25 to 1.75
- enc_beta: float32 [2, 320], P('section'), may hold values from -2 to 2
- dec_weight: bfloat16 [2, 3, 3, 640, 320], P('section'), may hold values from -0.078125 to 0.078125
- dec_bias: float32 [2, 320], P('section'), may hold values from -2 to 2
- dec_gain: float32 [2, 640], P('section'), may hold values from 0.25 to 1.75
- dec_beta: float32 [2, 640], P('section'), may hold values from -2 to 2
Outputs:
- encoded: bfloat16 [128, 16, 16, 320], P(('dp', 'section')), parts along dimension 0
- decoded: bfloat16 [128, 16, 16, 320], P(('dp', 'section')), parts along dimension 0
- queued: bfloat16 [128, 16, 16, 320], P(('dp', 'section')), parts along dimension 0
The draws below stay inside these ranges and needn't reach their ends.
There are 16 independent parts, one for each index of `dp`. The reference program is written for one: setup_inputs(seed, part) draws one part's arguments, and reference() takes and returns one part's arrays. A program takes and returns all parts, laid end to end along the dimension named above; an argument that names none is the same for every part. Nothing has to cross between parts.
All inputs are finite; a program needn't handle non-finite values.
Results may differ from the reference program's by a relative error of at most 0.0048.
Values may be sent and summed in bfloat16 or wider, within the bound.
A program may use at most 64 MiB of HBM per device.

```python
import jax
import jax.numpy as jnp
from jax import lax

C = 320
GROUPS = 32
SIDE = 16
TICKS = 2
IMG = 2
N_SECTION = 2


def block_scale(stream_key, shape, shards, least, high):
    def one(axis_at, blocks):
        heights = jax.random.uniform(jax.random.fold_in(jax.random.fold_in(stream_key, 6), axis_at), (blocks,), jnp.float32, least / len(shards), high / len(shards))
        return jnp.repeat(jnp.exp(heights), shape[axis_at] // blocks).reshape((-1,) + (1,) * (len(shape) - axis_at - 1))

    gain = one(*shards[0])
    for cut in shards[1:]:
        gain = gain * one(*cut)
    return gain


def noise(rng, dims, deviation, bound, cuts=(), kind=jnp.bfloat16):
    level = block_scale(rng, dims, cuts, -0.22, 0.18) if cuts else 1.0
    drawn = jax.random.normal(rng, dims, jnp.float32) * deviation * level
    return jnp.minimum(jnp.maximum(drawn, -bound), bound).astype(kind)


def setup_inputs(seed: int = 0, part: int = 0) -> dict:
    keys = jax.random.split(jax.random.key(seed), 13)
    part_splits = jax.random.split(jax.random.fold_in(keys[12], part), 13)
    enc_in = noise(part_splits[0], (N_SECTION * IMG, SIDE, SIDE, C), 1.0, 6.0, ((0, 2),))
    dec_in = noise(part_splits[1], (N_SECTION * IMG, SIDE, SIDE, C), 1.0, 6.0, ((0, 2),))
    fresh = noise(part_splits[2], ((TICKS - 1) * IMG, SIDE, SIDE, C), 1.0, 6.0)
    skip_queue = noise(part_splits[3], (N_SECTION * TICKS * IMG, SIDE, SIDE, C), 1.0, 6.0, ((0, 2),))
    enc_weight = noise(keys[4], (N_SECTION, 3, 3, C, C), (9 * C) ** -0.5, 0.109375, ((0, 2),))
    enc_bias = noise(keys[5], (N_SECTION, C), 0.3, 2.0, ((0, 2),), jnp.float32)
    enc_gain = jnp.clip(1.0 + 0.15 * jax.random.normal(keys[6], (N_SECTION, C), jnp.float32), 0.25, 1.75)
    enc_beta = noise(keys[7], (N_SECTION, C), 0.3, 2.0, ((0, 2),), jnp.float32)
    dec_weight = noise(keys[8], (N_SECTION, 3, 3, 2 * C, C), (18 * C) ** -0.5, 0.078125, ((0, 2),))
    dec_bias = noise(keys[9], (N_SECTION, C), 0.3, 2.0, ((0, 2),), jnp.float32)
    dec_gain = jnp.clip(1.0 + 0.15 * jax.random.normal(keys[10], (N_SECTION, 2 * C), jnp.float32), 0.25, 1.75)
    dec_beta = noise(keys[11], (N_SECTION, 2 * C), 0.3, 2.0, ((0, 2),), jnp.float32)
    return dict(enc_in=enc_in, dec_in=dec_in, fresh=fresh, skip_queue=skip_queue, enc_weight=enc_weight, enc_bias=enc_bias, enc_gain=enc_gain, enc_beta=enc_beta, dec_weight=dec_weight, dec_bias=dec_bias, dec_gain=dec_gain, dec_beta=dec_beta)


def norm_silu(values, norm_gain, norm_beta):
    layout = values.shape
    grouped = values.reshape(layout[:3] + (GROUPS, layout[3] // GROUPS))
    average = lax.optimization_barrier(jnp.mean(grouped, axis=(1, 2, 4), keepdims=True))
    centred = grouped - average
    variance = lax.optimization_barrier(jnp.mean(centred * centred, axis=(1, 2, 4), keepdims=True))
    normed = (centred * lax.rsqrt(variance + 1e-05)).reshape(layout)
    return jax.nn.silu(normed * norm_gain + norm_beta).astype(jnp.bfloat16)

def convolve(inputs, kernel):
    return lax.conv_general_dilated(inputs, kernel, (1, 1), 'SAME', dimension_numbers=('NHWC', 'HWIO', 'NHWC'), preferred_element_type=jnp.float32)

def encode(current, kernel, bias_row, norm_gain, norm_beta):
    widened = current.astype(jnp.float32)
    hidden = norm_silu(widened, norm_gain, norm_beta)
    return (widened + convolve(hidden, kernel) + bias_row).astype(jnp.bfloat16)

def decode(current, skipped, kernel, bias_row, norm_gain, norm_beta):
    joined = jnp.concatenate([current, skipped], axis=3).astype(jnp.float32)
    hidden = norm_silu(joined, norm_gain, norm_beta)
    return (current.astype(jnp.float32) + convolve(hidden, kernel) + bias_row).astype(jnp.bfloat16)

def reference(enc_in, dec_in, fresh, skip_queue, enc_weight, enc_bias, enc_gain, enc_beta, dec_weight, dec_bias, dec_gain, dec_beta):
    sections = N_SECTION
    map_dims = enc_in.shape[1:]
    images = enc_in.shape[0] // sections
    enc_now = enc_in.reshape((sections, images) + map_dims)
    dec_now = dec_in.reshape((sections, images) + map_dims)
    queue = skip_queue.reshape((sections, TICKS, images) + map_dims)
    arrivals = fresh.reshape((TICKS - 1, images) + map_dims)
    enc_list, dec_list, queue_list = ([], [], [])
    previous = None
    for turn_index in range(TICKS):
        skipped = queue[:, turn_index]
        if turn_index > 0:
            skipped = skipped.at[0].set(previous)
        enc_out = jax.vmap(encode)(enc_now, enc_weight, enc_bias, enc_gain, enc_beta)
        dec_out = jax.vmap(decode)(dec_now, skipped, dec_weight, dec_bias, dec_gain, dec_beta)
        received = enc_out[::-1]
        previous = received[0]
        enc_list.append(enc_out)
        dec_list.append(dec_out)
        queue_list.append(received)
        if turn_index + 1 < TICKS:
            enc_now = jnp.concatenate([arrivals[turn_index][None], enc_out[:-1]], axis=0)
            dec_now = jnp.concatenate([enc_out[-1:], dec_out[:-1]], axis=0)
    whole = (sections * TICKS * images,) + map_dims
    encoded = jnp.stack(enc_list, axis=1).reshape(whole)
    decoded = jnp.stack(dec_list, axis=1).reshape(whole)
    queued = jnp.stack(queue_list, axis=1).reshape(whole)
    return (encoded, decoded, queued)
```

```python
import functools

import jax
import jax.numpy as jnp
from jax import lax
from jax.experimental import pallas as pl
from jax.experimental.pallas import tpu as pltpu
from jax.sharding import PartitionSpec as P

GROUPS = 32
LANES = 256
F32 = jnp.float32
BF16 = jnp.bfloat16
MESH = pl.DeviceIdType.MESH


def membership(width, per_group):
    row = lax.broadcasted_iota(jnp.int32, (width, width), 0).astype(F32)
    column = lax.broadcasted_iota(jnp.int32, (width, width), 1).astype(F32)
    same = jnp.floor((row + 0.5) * (1.0 / per_group)) == jnp.floor((column + 0.5) * (1.0 / per_group))
    return jnp.where(same, 1.0, 0.0).astype(BF16)


def group_total(values, member):
    part = jnp.sum(values.reshape(values.shape[0] // 8, 8, values.shape[1]), axis=0)
    high = part.astype(BF16).astype(F32)
    rest = part - high
    middle = rest.astype(BF16).astype(F32)
    low = rest - middle
    pieces = jnp.concatenate([high, middle, low], axis=0).astype(BF16)
    return jnp.sum(jnp.dot(pieces, member, preferred_element_type=F32), axis=0, keepdims=True)


def norm_silu(values, member, per_group, gain, beta):
    share = 1.0 / (values.shape[0] * per_group)
    centred = values - group_total(values, member) * share
    variance = group_total(centred * centred, member) * share
    half = centred * (lax.rsqrt(variance + 1e-05) * (0.5 * gain)) + 0.5 * beta
    return half + half * jnp.tanh(half)


def spread(buffer, values, side, pitch, offset):
    rows, width = values.shape
    cell = lax.rem(lax.broadcasted_iota(jnp.int32, (rows, width), 0), side)
    before = jnp.where(cell == 0, 0.0, pltpu.roll(values, 1, 0))
    after = jnp.where(cell == side - 1, 0.0, pltpu.roll(values, rows - 1, 0))
    for tap, moved in enumerate((before, values, after)):
        at = tap * pitch + offset
        buffer[side : side + rows, at : at + width] = moved.astype(BF16)


def conv_add(out, start, buffer, weight, tail, source, bias, side):
    rows, width = source.shape
    wide = width // LANES * LANES
    narrow = width - wide
    total = source[:, :wide] + bias[:, :wide]
    for tap in range(3):
        total += jnp.dot(
            buffer[tap * side : tap * side + rows, :], weight[tap, :, :wide], preferred_element_type=F32
        )
    out[start : start + rows, :wide] = total.astype(BF16)
    ends = jnp.dot(buffer[...], tail[...], preferred_element_type=F32)
    total = source[:, wide:] + bias[:, wide:]
    for tap in range(3):
        total += ends[tap * side : tap * side + rows, tap * narrow : (tap + 1) * narrow]
    out[start : start + rows, wide:] = total.astype(BF16)


def relay(sections, ticks, images, side, *refs):
    (enc_in, dec_in, fresh, queue, enc_w, enc_b, enc_g, enc_o, dec_w, dec_b, dec_g, dec_o) = refs[:12]
    (encoded, decoded, queued) = refs[12:15]
    (e0, d0, fr, sk, we, be, ge, oe, wd, bd, gd, od) = refs[15:27]
    (enc_out, dec_out, q_buf, e_buf, d_buf, enc_cols, dec_cols, enc_tail, dec_tail) = refs[27:36]
    (load_sem, store_sem, q_send, q_recv, e_send, e_recv, d_send, d_recv) = refs[36:]
    me = lax.axis_index("section")
    mirror = sections - 1 - me
    rows = side * side
    channels = e0.shape[1]

    barrier = pltpu.get_barrier_semaphore()
    pl.semaphore_signal(barrier, inc=1, device_id={"section": mirror}, device_id_type=MESH)
    if sections > 2:
        behind = jnp.logical_and(me > 0, me - 1 != mirror)
        ahead = jnp.logical_and(me < sections - 1, me + 1 != mirror)

        @pl.when(behind)
        def _():
            pl.semaphore_signal(barrier, inc=1, device_id={"section": me - 1}, device_id_type=MESH)

    loads = []
    for source, target in (
        (enc_in, e0), (enc_g, ge), (enc_o, oe), (enc_w, we), (enc_b, be), (dec_in, d0), (queue, sk),
        (dec_g, gd), (dec_o, od), (dec_w, wd), (dec_b, bd), (fresh, fr),
    ):
        copy = pltpu.make_async_copy(source, target, load_sem.at[len(loads)])
        copy.start()
        loads.append(copy)

    def span(tick, image):
        return pl.ds((tick * images + image) * rows, rows)

    def store(source, target, slot):
        return pltpu.make_async_copy(source, target, store_sem.at[slot])

    def to_mirror(tick, image):
        last = tick == ticks - 1
        return pltpu.make_async_remote_copy(
            src_ref=enc_out.at[span(tick, image)],
            dst_ref=(queued if last else q_buf).at[span(tick, image)],
            send_sem=q_send.at[tick * images + image],
            recv_sem=q_recv.at[tick * images + image],
            device_id={"section": mirror},
            device_id_type=MESH,
        )

    def to_next(source, target, send, recv, tick, image):
        return pltpu.make_async_remote_copy(
            src_ref=source.at[span(tick, image)],
            dst_ref=target.at[span(tick, image)],
            send_sem=send.at[tick * images + image],
            recv_sem=recv.at[tick * images + image],
            device_id={"section": lax.rem(me + 1, sections)},
            device_id_type=MESH,
        )

    enc_next = functools.partial(to_next, enc_out, e_buf, e_send, e_recv)
    dec_next = functools.partial(to_next, dec_out, d_buf, d_send, d_recv)

    enc_member = membership(channels, channels // GROUPS)
    dec_member = membership(channels, 2 * channels // GROUPS)
    for columns in (enc_cols, dec_cols):
        edge = jnp.zeros((images, side, columns.shape[2]), BF16)
        columns[:, :side, :] = edge
        columns[:, side + rows :, :] = edge
    wide = channels // LANES * LANES
    narrow = channels - wide
    stores = []

    for tick in range(ticks):
        for image in range(images):
            if tick == 0 and image == 0:
                for copy in loads[:3]:
                    copy.wait()
            place = span(tick, image)
            if tick == 0:
                current = e0[image * rows : (image + 1) * rows, :].astype(F32)
            else:
                if image == 0 and tick == 1:
                    loads[11].wait()
                past = span(tick - 1, image)
                to_mirror(tick - 1, image).wait_recv()
                keep = store(q_buf.at[past], queued.at[past], len(stores))
                keep.start()
                stores.append(keep)
                moved = q_buf[past, :].astype(F32)
                if sections > 2:

                    @pl.when(behind)
                    def _():
                        enc_next(tick - 1, image).wait_recv()

                    moved = jnp.where(me - 1 == mirror, moved, e_buf[past, :].astype(F32))
                current = jnp.where(me == 0, fr[past, :].astype(F32), moved)
            hidden = norm_silu(current, enc_member, channels // GROUPS, ge[...], oe[...])
            spread(enc_cols.at[image], hidden, side, channels, 0)
            if tick == 0 and image == 0:
                for copy in loads[3:5]:
                    copy.wait()
                for tap in range(3):
                    enc_tail[:, tap * narrow : (tap + 1) * narrow] = we[tap, :, wide:]
            conv_add(
                enc_out, (tick * images + image) * rows, enc_cols.at[image], we, enc_tail, current, be[...], side
            )
            if tick == 0 and image == 0:
                pl.semaphore_wait(barrier, 1)
                if sections > 2:

                    @pl.when(ahead)
                    def _():
                        pl.semaphore_wait(barrier, 1)

            to_mirror(tick, image).start()
            if sections > 2 and tick < ticks - 1:

                @pl.when(ahead)
                def _():
                    enc_next(tick, image).start()

            keep = store(enc_out.at[place], encoded.at[place], len(stores))
            keep.start()
            stores.append(keep)

        for image in range(images):
            if tick == 0 and image == 0:
                for copy in loads[5:9]:
                    copy.wait()
            place = span(tick, image)
            skipped = sk[place, :].astype(F32)
            if tick == 0:
                current = d0[image * rows : (image + 1) * rows, :].astype(F32)
            else:
                past = span(tick - 1, image)

                @pl.when(me > 0)
                def _():
                    dec_next(tick - 1, image).wait_recv()

                moved = q_buf[past, :].astype(F32)
                current = jnp.where(me == 0, moved, d_buf[past, :].astype(F32))
                skipped = jnp.where(me == 0, moved, skipped)
            for half, values in enumerate((current, skipped)):
                lanes = slice(half * channels, (half + 1) * channels)
                hidden = norm_silu(values, dec_member, 2 * channels // GROUPS, gd[:, lanes], od[:, lanes])
                spread(dec_cols.at[image], hidden, side, 2 * channels, half * channels)
            if tick == 0 and image == 0:
                for copy in loads[9:11]:
                    copy.wait()
                for tap in range(3):
                    dec_tail[:, tap * narrow : (tap + 1) * narrow] = wd[tap, :, wide:]
            conv_add(
                dec_out, (tick * images + image) * rows, dec_cols.at[image], wd, dec_tail, current, bd[...], side
            )
            if tick < ticks - 1:

                @pl.when(me < sections - 1)
                def _():
                    dec_next(tick, image).start()

            keep = store(dec_out.at[place], decoded.at[place], len(stores))
            keep.start()
            stores.append(keep)

    for keep in stores:
        keep.wait()
    for tick in range(ticks):
        for image in range(images):
            to_mirror(tick, image).wait_send()
            if tick == ticks - 1:
                to_mirror(tick, image).wait_recv()
            else:
                if sections > 2:

                    @pl.when(ahead)
                    def _():
                        enc_next(tick, image).wait_send()

                @pl.when(me < sections - 1)
                def _():
                    dec_next(tick, image).wait_send()


def shards(sections, enc_in, dec_in, fresh, skip_queue, enc_weight, enc_bias, enc_gain, enc_beta,
           dec_weight, dec_bias, dec_gain, dec_beta):
    images, side, _, channels = enc_in.shape
    ticks = skip_queue.shape[0] // images
    rows = side * side

    def flat(maps):
        return maps.reshape(maps.shape[0] * rows, channels)

    def taps(kernel):
        return kernel.reshape(3, 3 * kernel.shape[3], channels)

    operands = (
        flat(enc_in), flat(dec_in), flat(fresh), flat(skip_queue),
        taps(enc_weight), enc_bias, enc_gain, enc_beta,
        taps(dec_weight), dec_bias, dec_gain, dec_beta,
    )
    total = ticks * images * rows
    maps = jax.ShapeDtypeStruct((total, channels), BF16)
    narrow = channels % LANES
    steps = ticks * images
    anywhere = pl.BlockSpec(memory_space=pl.ANY)
    outs = pl.pallas_call(
        functools.partial(relay, sections, ticks, images, side),
        out_shape=(maps, maps, maps),
        in_specs=[anywhere] * len(operands),
        out_specs=[anywhere] * 3,
        scratch_shapes=[pltpu.VMEM(value.shape, value.dtype) for value in operands]
        + [
            pltpu.VMEM((total, channels), BF16),
            pltpu.VMEM((total, channels), BF16),
            pltpu.VMEM((total, channels), BF16),
            pltpu.VMEM((total if sections > 2 else 16, channels), BF16),
            pltpu.VMEM((total, channels), BF16),
            pltpu.VMEM((images, rows + 2 * side, 3 * channels), BF16),
            pltpu.VMEM((images, rows + 2 * side, 6 * channels), BF16),
            pltpu.VMEM((3 * channels, 3 * narrow), BF16),
            pltpu.VMEM((6 * channels, 3 * narrow), BF16),
            pltpu.SemaphoreType.DMA((len(operands),)),
            pltpu.SemaphoreType.DMA((3 * steps,)),
        ]
        + [pltpu.SemaphoreType.DMA((steps,))] * 6,
        compiler_params=pltpu.CompilerParams(
            collective_id=0, has_side_effects=True, vmem_limit_bytes=56 * 1024 * 1024
        ),
        cost_estimate=pl.CostEstimate(
            flops=steps * rows * 2 * 27 * channels * channels, bytes_accessed=12 * 1024 * 1024, transcendentals=0
        ),
    )(*operands)
    return tuple(out.reshape(ticks * images, side, side, channels) for out in outs)


def solution(mesh):
    maps = P(("dp", "section"), None, None, None)
    row = P("section", None)
    kernel = P("section", None, None, None, None)
    in_specs = (maps, maps, P("dp", None, None, None), maps, kernel, row, row, row, kernel, row, row, row)
    return jax.shard_map(
        functools.partial(shards, mesh.shape["section"]),
        mesh=mesh,
        in_specs=in_specs,
        out_specs=(maps, maps, maps),
        check_vma=False,
    )
```

```python
import functools

import jax
import jax.numpy as jnp
from jax import lax
from jax.experimental import pallas as pl
from jax.experimental.pallas import tpu as pltpu
from jax.sharding import PartitionSpec as P

GROUPS = 32
LANES = 256
F32 = jnp.float32
BF16 = jnp.bfloat16
MESH = pl.DeviceIdType.MESH


def membership(width, per_group):
    row = lax.broadcasted_iota(jnp.int32, (width, width), 0).astype(F32)
    column = lax.broadcasted_iota(jnp.int32, (width, width), 1).astype(F32)
    same = jnp.floor((row + 0.5) * (1.0 / per_group)) == jnp.floor((column + 0.5) * (1.0 / per_group))
    return jnp.where(same, 1.0, 0.0).astype(BF16)


def group_total(values, member):
    part = jnp.sum(values.reshape(values.shape[0] // 8, 8, values.shape[1]), axis=0)
    high = part.astype(BF16).astype(F32)
    rest = part - high
    middle = rest.astype(BF16).astype(F32)
    low = rest - middle
    pieces = jnp.concatenate([high, middle, low], axis=0).astype(BF16)
    return jnp.sum(jnp.dot(pieces, member, preferred_element_type=F32), axis=0, keepdims=True)


def norm_silu(values, member, per_group, gain, beta):
    share = 1.0 / (values.shape[0] * per_group)
    centred = values - group_total(values, member) * share
    variance = group_total(centred * centred, member) * share
    half = centred * (lax.rsqrt(variance + 1e-05) * (0.5 * gain)) + 0.5 * beta
    return half + half * jnp.tanh(half)


def spread(buffer, values, side, pitch, offset):
    rows, width = values.shape
    cell = lax.rem(lax.broadcasted_iota(jnp.int32, (rows, width), 0), side)
    before = jnp.where(cell == 0, 0.0, pltpu.roll(values, 1, 0))
    after = jnp.where(cell == side - 1, 0.0, pltpu.roll(values, rows - 1, 0))
    for tap, moved in enumerate((before, values, after)):
        at = tap * pitch + offset
        buffer[side : side + rows, at : at + width] = moved.astype(BF16)


def product(left, right, flipped):
    return lax.dot_general(left, right, (((1,), (1 if flipped else 0,)), ((), ())), preferred_element_type=F32)


def pack(target, start, wide, tail):
    rows, narrow = tail.shape
    depth = rows * narrow // wide.shape[1]
    target[start : start + rows, :] = wide
    for part in range(rows // depth):
        target[start + rows : start + rows + depth, part * narrow : (part + 1) * narrow] = tail[
            part * depth : (part + 1) * depth, :
        ]


def unpack(source, start, rows, narrow):
    depth = rows * narrow // source.shape[1]
    tail = [
        source[start + rows : start + rows + depth, part * narrow : (part + 1) * narrow]
        for part in range(rows // depth)
    ]
    return source[start : start + rows, :], jnp.concatenate(tail, axis=0)


def conv_add(out, packed, step, buffer, weight, tail, flipped, source, bias, side):
    rows, width = source.shape
    start = step * rows
    wide = width // LANES * LANES
    narrow = width - wide
    total = source[:, :wide] + bias[:, :wide]
    for tap in range(3):
        total += product(
            buffer[tap * side : tap * side + rows, :], weight[tap] if flipped else weight[tap, :, :wide], flipped
        )
    main = total.astype(BF16)
    out[start : start + rows, :wide] = main
    ends = product(buffer[...], tail[...], flipped)
    total = source[:, wide:] + bias[:, wide:]
    for tap in range(3):
        total += ends[tap * side : tap * side + rows, tap * narrow : (tap + 1) * narrow]
    rest = total.astype(BF16)
    out[start : start + rows, wide:] = rest
    pack(packed, step * packed.shape[0] // (out.shape[0] // rows), main, rest)


def relay(sections, ticks, images, side, *refs):
    (enc_in, dec_in, fresh, queue, enc_w, enc_b, enc_g, enc_o, dec_w, dec_b, dec_g, dec_o) = refs[:12]
    (encoded, decoded, queued) = refs[12:15]
    (e0, d0, fr, sk, we, be, ge, oe, wd, bd, gd, od) = refs[15:27]
    (enc_out, dec_out, q_out, enc_pack, dec_pack, q_buf, e_buf, d_buf) = refs[27:35]
    (enc_cols, dec_cols, enc_tail, dec_tail) = refs[35:39]
    (load_sem, store_sem, q_send, q_recv, e_send, e_recv, d_send, d_recv) = refs[39:]
    me = lax.axis_index("section")
    mirror = sections - 1 - me
    rows = side * side
    channels = e0.shape[1]
    wide = channels // LANES * LANES
    narrow = channels - wide
    packed = rows * channels // wide

    barrier = pltpu.get_barrier_semaphore()
    pl.semaphore_signal(barrier, inc=1, device_id={"section": mirror}, device_id_type=MESH)
    if sections > 2:
        behind = jnp.logical_and(me > 0, me - 1 != mirror)
        ahead = jnp.logical_and(me < sections - 1, me + 1 != mirror)

        @pl.when(behind)
        def _():
            pl.semaphore_signal(barrier, inc=1, device_id={"section": me - 1}, device_id_type=MESH)

    loads = []
    moves = [
        (enc_in, e0), (enc_g, ge), (enc_o, oe), (enc_w, we), (enc_b, be), (dec_in, d0), (queue, sk),
        (dec_g, gd), (dec_o, od), (dec_b, bd), (fresh, fr),
    ]
    for tap in range(9):
        lanes = pl.ds(tap % 3 * 2 * channels, 2 * channels)
        source = dec_w.at[tap]
        moves.append((source.at[pl.ds(0, wide)], wd.at[tap // 3, :, lanes]))
        moves.append((source.at[pl.ds(wide, narrow)], dec_tail.at[pl.ds(tap // 3 * narrow, narrow), lanes]))
    for source, target in moves:
        copy = pltpu.make_async_copy(source, target, load_sem.at[len(loads)])
        copy.start()
        loads.append(copy)

    def span(tick, image):
        return pl.ds((tick * images + image) * rows, rows)

    def store(source, target, slot):
        return pltpu.make_async_copy(source, target, store_sem.at[slot])

    def bundle(tick, image):
        return pl.ds((tick * images + image) * packed, packed)

    def opened(source, tick, image):
        return unpack(source, (tick * images + image) * packed, rows, narrow)

    def joined(source, tick, image):
        return jnp.concatenate([part.astype(F32) for part in opened(source, tick, image)], axis=1)

    def keep_mirrored(tick, image):
        main, rest = opened(q_buf, tick, image)
        start = (tick * images + image) * rows
        q_out[start : start + rows, :wide] = main
        q_out[start : start + rows, wide:] = rest
        keep = store(q_out.at[span(tick, image)], queued.at[span(tick, image)], len(stores))
        keep.start()
        stores.append(keep)

    def to_mirror(tick, image):
        return pltpu.make_async_remote_copy(
            src_ref=enc_pack.at[bundle(tick, image)],
            dst_ref=q_buf.at[bundle(tick, image)],
            send_sem=q_send.at[tick * images + image],
            recv_sem=q_recv.at[tick * images + image],
            device_id={"section": mirror},
            device_id_type=MESH,
        )

    def to_next(source, target, send, recv, tick, image):
        return pltpu.make_async_remote_copy(
            src_ref=source.at[bundle(tick, image)],
            dst_ref=target.at[bundle(tick, image)],
            send_sem=send.at[tick * images + image],
            recv_sem=recv.at[tick * images + image],
            device_id={"section": lax.rem(me + 1, sections)},
            device_id_type=MESH,
        )

    enc_next = functools.partial(to_next, enc_pack, e_buf, e_send, e_recv)
    dec_next = functools.partial(to_next, dec_pack, d_buf, d_send, d_recv)

    enc_member = membership(channels, channels // GROUPS)
    dec_member = membership(channels, 2 * channels // GROUPS)
    for columns in (enc_cols, dec_cols):
        edge = jnp.zeros((images, side, columns.shape[2]), BF16)
        columns[:, :side, :] = edge
        columns[:, side + rows :, :] = edge
    stores = []

    for tick in range(ticks):
        for image in range(images):
            if tick == 0 and image == 0:
                for copy in loads[:3]:
                    copy.wait()
            place = span(tick, image)
            if tick == 0:
                current = e0[image * rows : (image + 1) * rows, :].astype(F32)
            else:
                if image == 0 and tick == 1:
                    loads[10].wait()
                past = span(tick - 1, image)
                to_mirror(tick - 1, image).wait_recv()
                keep_mirrored(tick - 1, image)
                moved = joined(q_buf, tick - 1, image)
                if sections > 2:

                    @pl.when(behind)
                    def _():
                        enc_next(tick - 1, image).wait_recv()

                    moved = jnp.where(me - 1 == mirror, moved, joined(e_buf, tick - 1, image))
                current = jnp.where(me == 0, fr[past, :].astype(F32), moved)
            hidden = norm_silu(current, enc_member, channels // GROUPS, ge[...], oe[...])
            spread(enc_cols.at[image], hidden, side, channels, 0)
            if tick == 0 and image == 0:
                for copy in loads[3:5]:
                    copy.wait()
                for tap in range(3):
                    enc_tail[:, tap * narrow : (tap + 1) * narrow] = we[tap, :, wide:]
            conv_add(
                enc_out, enc_pack, tick * images + image, enc_cols.at[image], we, enc_tail, False, current, be[...],
                side,
            )
            if tick == 0 and image == 0:
                pl.semaphore_wait(barrier, 1)
                if sections > 2:

                    @pl.when(ahead)
                    def _():
                        pl.semaphore_wait(barrier, 1)

            to_mirror(tick, image).start()
            if sections > 2 and tick < ticks - 1:

                @pl.when(ahead)
                def _():
                    enc_next(tick, image).start()

            keep = store(enc_out.at[place], encoded.at[place], len(stores))
            keep.start()
            stores.append(keep)

        for image in range(images):
            if tick == 0 and image == 0:
                for copy in loads[5:9]:
                    copy.wait()
            place = span(tick, image)
            skipped = sk[place, :].astype(F32)
            if tick == 0:
                current = d0[image * rows : (image + 1) * rows, :].astype(F32)
            else:

                @pl.when(me > 0)
                def _():
                    dec_next(tick - 1, image).wait_recv()

                moved = joined(q_buf, tick - 1, image)
                current = jnp.where(me == 0, moved, joined(d_buf, tick - 1, image))
                skipped = jnp.where(me == 0, moved, skipped)
            for half, values in enumerate((current, skipped)):
                lanes = slice(half * channels, (half + 1) * channels)
                hidden = norm_silu(values, dec_member, 2 * channels // GROUPS, gd[:, lanes], od[:, lanes])
                spread(dec_cols.at[image], hidden, side, 2 * channels, half * channels)
            if tick == 0 and image == 0:
                for copy in loads[9:10] + loads[11:]:
                    copy.wait()
            conv_add(
                dec_out, dec_pack, tick * images + image, dec_cols.at[image], wd, dec_tail, True, current, bd[...],
                side,
            )
            if tick < ticks - 1:

                @pl.when(me < sections - 1)
                def _():
                    dec_next(tick, image).start()

            keep = store(dec_out.at[place], decoded.at[place], len(stores))
            keep.start()
            stores.append(keep)

    for image in range(images):
        to_mirror(ticks - 1, image).wait_recv()
        keep_mirrored(ticks - 1, image)
    for keep in stores:
        keep.wait()
    for tick in range(ticks):
        for image in range(images):
            to_mirror(tick, image).wait_send()
            if tick < ticks - 1:
                if sections > 2:

                    @pl.when(ahead)
                    def _():
                        enc_next(tick, image).wait_send()

                @pl.when(me < sections - 1)
                def _():
                    dec_next(tick, image).wait_send()


def hand_on(*refs):
    count = len(refs) // 2
    copies = []
    for source, target in zip(refs[:count], refs[count:-1]):
        half = source.shape[0] // 2
        for part in range(2):
            at = pl.ds(part * half, half)
            copies.append(pltpu.make_async_copy(source.at[at], target.at[at], refs[-1].at[len(copies)]))
    for copy in copies:
        copy.start()
    for copy in copies:
        copy.wait()


def shards(sections, enc_in, dec_in, fresh, skip_queue, enc_weight, enc_bias, enc_gain, enc_beta,
           dec_weight, dec_bias, dec_gain, dec_beta):
    images, side, _, channels = enc_in.shape
    ticks = skip_queue.shape[0] // images
    rows = side * side

    def flat(maps):
        return maps.reshape(maps.shape[0] * rows, channels)

    def taps(kernel):
        return kernel.reshape(3, 3 * channels, channels)

    operands = (
        flat(enc_in), flat(dec_in), flat(fresh), flat(skip_queue),
        taps(enc_weight), enc_bias, enc_gain, enc_beta,
        lax.transpose(dec_weight, (0, 1, 2, 4, 3)).reshape(9, channels, 2 * channels), dec_bias, dec_gain, dec_beta,
    )
    total = ticks * images * rows
    maps = jax.ShapeDtypeStruct((total, channels), BF16)
    narrow = channels % LANES
    wide = channels - narrow
    packed = pltpu.VMEM((ticks * images * rows * channels // wide, wide), BF16)
    spare = packed if sections > 2 else pltpu.VMEM((16, wide), BF16)
    held = [pltpu.VMEM(value.shape, value.dtype) for value in operands]
    held[8] = pltpu.VMEM((3, wide, 6 * channels), BF16)
    steps = ticks * images
    anywhere = pl.BlockSpec(memory_space=pl.ANY)
    outs = pl.pallas_call(
        functools.partial(relay, sections, ticks, images, side),
        out_shape=(pltpu.VMEM(maps.shape, maps.dtype),) * 3,
        in_specs=[anywhere] * len(operands),
        out_specs=[anywhere] * 3,
        scratch_shapes=held
        + [
            pltpu.VMEM((total, channels), BF16),
            pltpu.VMEM((total, channels), BF16),
            pltpu.VMEM((total, channels), BF16),
            packed,
            packed,
            packed,
            spare,
            packed,
            pltpu.VMEM((images, rows + 2 * side, 3 * channels), BF16),
            pltpu.VMEM((images, rows + 2 * side, 6 * channels), BF16),
            pltpu.VMEM((3 * channels, 3 * narrow), BF16),
            pltpu.VMEM((3 * narrow, 6 * channels), BF16),
            pltpu.SemaphoreType.DMA((len(operands) + 17,)),
            pltpu.SemaphoreType.DMA((3 * steps,)),
        ]
        + [pltpu.SemaphoreType.DMA((steps,))] * 6,
        compiler_params=pltpu.CompilerParams(
            collective_id=0, has_side_effects=True, vmem_limit_bytes=56 * 1024 * 1024
        ),
        cost_estimate=pl.CostEstimate(
            flops=steps * rows * 2 * 27 * channels * channels, bytes_accessed=12 * 1024 * 1024, transcendentals=0
        ),
    )(*operands)
    outs = pl.pallas_call(
        hand_on,
        out_shape=(maps, maps, maps),
        in_specs=[anywhere] * 3,
        out_specs=[anywhere] * 3,
        scratch_shapes=[pltpu.SemaphoreType.DMA((6,))],
    )(*outs)
    return tuple(out.reshape(ticks * images, side, side, channels) for out in outs)


def solution(mesh):
    maps = P(("dp", "section"), None, None, None)
    row = P("section", None)
    kernel = P("section", None, None, None, None)
    in_specs = (maps, maps, P("dp", None, None, None), maps, kernel, row, row, row, kernel, row, row, row)
    return jax.shard_map(
        functools.partial(shards, mesh.shape["section"]),
        mesh=mesh,
        in_specs=in_specs,
        out_specs=(maps, maps, maps),
        check_vma=False,
    )
```

```python
import functools

import jax
import jax.numpy as jnp
from jax import lax
from jax.experimental import pallas as pl
from jax.experimental.pallas import tpu as pltpu
from jax.sharding import PartitionSpec as P

GROUPS = 32
LANES = 256
F32 = jnp.float32
BF16 = jnp.bfloat16
MESH = pl.DeviceIdType.MESH


def membership(width, per_group):
    row = lax.broadcasted_iota(jnp.int32, (width, width), 0).astype(F32)
    column = lax.broadcasted_iota(jnp.int32, (width, width), 1).astype(F32)
    same = jnp.floor((row + 0.5) * (1.0 / per_group)) == jnp.floor((column + 0.5) * (1.0 / per_group))
    return jnp.where(same, 1.0, 0.0).astype(BF16)


def group_total(values, member):
    part = jnp.sum(values.reshape(values.shape[0] // 8, 8, values.shape[1]), axis=0)
    high = part.astype(BF16).astype(F32)
    rest = part - high
    middle = rest.astype(BF16).astype(F32)
    low = rest - middle
    pieces = jnp.concatenate([high, middle, low], axis=0).astype(BF16)
    return jnp.sum(jnp.dot(pieces, member, preferred_element_type=F32), axis=0, keepdims=True)


def norm_silu(values, member, per_group, gain, beta):
    share = 1.0 / (values.shape[0] * per_group)
    centred = values - group_total(values, member) * share
    variance = group_total(centred * centred, member) * share
    half = centred * (lax.rsqrt(variance + 1e-05) * (0.5 * gain)) + 0.5 * beta
    return half + half * jnp.tanh(half)


def spread(buffer, values, side, pitch, offset):
    rows, width = values.shape
    cell = lax.rem(lax.broadcasted_iota(jnp.int32, (rows, width), 0), side)
    before = jnp.where(cell == 0, 0.0, pltpu.roll(values, 1, 0))
    after = jnp.where(cell == side - 1, 0.0, pltpu.roll(values, rows - 1, 0))
    for tap, moved in enumerate((before, values, after)):
        at = tap * pitch + offset
        buffer[side : side + rows, at : at + width] = moved.astype(BF16)


def product(left, right, flipped):
    return lax.dot_general(left, right, (((1,), (1 if flipped else 0,)), ((), ())), preferred_element_type=F32)


def pack(target, start, wide, tail):
    rows, narrow = tail.shape
    depth = rows * narrow // wide.shape[1]
    target[start : start + rows, :] = wide
    for part in range(rows // depth):
        target[start + rows : start + rows + depth, part * narrow : (part + 1) * narrow] = tail[
            part * depth : (part + 1) * depth, :
        ]


def unpack(source, start, rows, narrow):
    depth = rows * narrow // source.shape[1]
    tail = [
        source[start + rows : start + rows + depth, part * narrow : (part + 1) * narrow]
        for part in range(rows // depth)
    ]
    return source[start : start + rows, :], jnp.concatenate(tail, axis=0)


def conv_add(out, packed, step, buffer, weight, tail, flipped, source, bias, side):
    rows, width = source.shape
    start = step * rows
    wide = width // LANES * LANES
    narrow = width - wide
    total = source[:, :wide] + bias[:, :wide]
    for tap in range(3):
        total += product(
            buffer[tap * side : tap * side + rows, :], weight[tap] if flipped else weight[tap, :, :wide], flipped
        )
    main = total.astype(BF16)
    out[start : start + rows, :wide] = main
    ends = product(buffer[...], tail[...], flipped)
    total = source[:, wide:] + bias[:, wide:]
    for tap in range(3):
        total += ends[tap * side : tap * side + rows, tap * narrow : (tap + 1) * narrow]
    rest = total.astype(BF16)
    out[start : start + rows, wide:] = rest
    pack(packed, step * packed.shape[0] // (out.shape[0] // rows), main, rest)


def relay(sections, ticks, images, side, *refs):
    (enc_in, dec_in, fresh, queue, enc_w, enc_b, enc_g, enc_o, dec_w, dec_b, dec_g, dec_o) = refs[:12]
    (encoded, decoded, queued) = refs[12:15]
    (e0, d0, fr, sk, we, be, ge, oe, wd, bd, gd, od) = refs[15:27]
    (enc_pack, dec_pack, q_buf, e_buf, d_buf, enc_cols, dec_cols, enc_tail, dec_tail) = refs[27:36]
    (load_sem, q_send, q_recv, e_send, e_recv, d_send, d_recv) = refs[36:]
    me = lax.axis_index("section")
    mirror = sections - 1 - me
    rows = side * side
    channels = e0.shape[1]
    wide = channels // LANES * LANES
    narrow = channels - wide
    packed = rows * channels // wide

    barrier = pltpu.get_barrier_semaphore()
    pl.semaphore_signal(barrier, inc=1, device_id={"section": mirror}, device_id_type=MESH)
    if sections > 2:
        behind = jnp.logical_and(me > 0, me - 1 != mirror)
        ahead = jnp.logical_and(me < sections - 1, me + 1 != mirror)

        @pl.when(behind)
        def _():
            pl.semaphore_signal(barrier, inc=1, device_id={"section": me - 1}, device_id_type=MESH)

    loads = []
    moves = [
        (enc_in, e0), (enc_g, ge), (enc_o, oe), (enc_w, we), (enc_b, be), (dec_in, d0), (queue, sk),
        (dec_g, gd), (dec_o, od), (dec_b, bd), (fresh, fr),
    ]
    for tap in range(9):
        lanes = pl.ds(tap % 3 * 2 * channels, 2 * channels)
        source = dec_w.at[tap]
        moves.append((source.at[pl.ds(0, wide)], wd.at[tap // 3, :, lanes]))
        moves.append((source.at[pl.ds(wide, narrow)], dec_tail.at[pl.ds(tap // 3 * narrow, narrow), lanes]))
    for source, target in moves:
        copy = pltpu.make_async_copy(source, target, load_sem.at[len(loads)])
        loads.append(copy)
    for copy in loads[:5]:
        copy.start()

    def span(tick, image):
        return pl.ds((tick * images + image) * rows, rows)

    def bundle(tick, image):
        return pl.ds((tick * images + image) * packed, packed)

    def opened(source, tick, image):
        return unpack(source, (tick * images + image) * packed, rows, narrow)

    def joined(source, tick, image):
        return jnp.concatenate([part.astype(F32) for part in opened(source, tick, image)], axis=1)

    def keep_mirrored(tick, image):
        main, rest = opened(q_buf, tick, image)
        start = (tick * images + image) * rows
        queued[start : start + rows, :wide] = main
        queued[start : start + rows, wide:] = rest

    def to_mirror(tick, image):
        return pltpu.make_async_remote_copy(
            src_ref=enc_pack.at[bundle(tick, image)],
            dst_ref=q_buf.at[bundle(tick, image)],
            send_sem=q_send.at[tick * images + image],
            recv_sem=q_recv.at[tick * images + image],
            device_id={"section": mirror},
            device_id_type=MESH,
        )

    def to_next(source, target, send, recv, tick, image):
        return pltpu.make_async_remote_copy(
            src_ref=source.at[bundle(tick, image)],
            dst_ref=target.at[bundle(tick, image)],
            send_sem=send.at[tick * images + image],
            recv_sem=recv.at[tick * images + image],
            device_id={"section": lax.rem(me + 1, sections)},
            device_id_type=MESH,
        )

    enc_next = functools.partial(to_next, enc_pack, e_buf, e_send, e_recv)
    dec_next = functools.partial(to_next, dec_pack, d_buf, d_send, d_recv)

    enc_member = membership(channels, channels // GROUPS)
    dec_member = membership(channels, 2 * channels // GROUPS)
    for columns in (enc_cols, dec_cols):
        edge = jnp.zeros((images, side, columns.shape[2]), BF16)
        columns[:, :side, :] = edge
        columns[:, side + rows :, :] = edge

    for tick in range(ticks):
        for image in range(images):
            if tick == 0 and image == 0:
                for copy in loads[:3]:
                    copy.wait()
            place = span(tick, image)
            if tick == 0:
                current = e0[image * rows : (image + 1) * rows, :].astype(F32)
            else:
                if image == 0 and tick == 1:
                    loads[10].wait()
                past = span(tick - 1, image)
                to_mirror(tick - 1, image).wait_recv()
                keep_mirrored(tick - 1, image)
                moved = joined(q_buf, tick - 1, image)
                if sections > 2:

                    @pl.when(behind)
                    def _():
                        enc_next(tick - 1, image).wait_recv()

                    moved = jnp.where(me - 1 == mirror, moved, joined(e_buf, tick - 1, image))
                current = jnp.where(me == 0, fr[past, :].astype(F32), moved)
            hidden = norm_silu(current, enc_member, channels // GROUPS, ge[...], oe[...])
            spread(enc_cols.at[image], hidden, side, channels, 0)
            if tick == 0 and image == 0:
                for copy in loads[3:5]:
                    copy.wait()
                for copy in loads[5:]:
                    copy.start()
                for tap in range(3):
                    enc_tail[:, tap * narrow : (tap + 1) * narrow] = we[tap, :, wide:]
            conv_add(
                encoded, enc_pack, tick * images + image, enc_cols.at[image], we, enc_tail, False, current, be[...],
                side,
            )
            if tick == 0 and image == 0:
                pl.semaphore_wait(barrier, 1)
                if sections > 2:

                    @pl.when(ahead)
                    def _():
                        pl.semaphore_wait(barrier, 1)

            to_mirror(tick, image).start()
            if sections > 2 and tick < ticks - 1:

                @pl.when(ahead)
                def _():
                    enc_next(tick, image).start()

        for image in range(images):
            if tick == 0 and image == 0:
                for copy in loads[5:9]:
                    copy.wait()
            place = span(tick, image)
            skipped = sk[place, :].astype(F32)
            if tick == 0:
                current = d0[image * rows : (image + 1) * rows, :].astype(F32)
            else:

                @pl.when(me > 0)
                def _():
                    dec_next(tick - 1, image).wait_recv()

                moved = joined(q_buf, tick - 1, image)
                current = jnp.where(me == 0, moved, joined(d_buf, tick - 1, image))
                skipped = jnp.where(me == 0, moved, skipped)
            for half, values in enumerate((current, skipped)):
                lanes = slice(half * channels, (half + 1) * channels)
                hidden = norm_silu(values, dec_member, 2 * channels // GROUPS, gd[:, lanes], od[:, lanes])
                spread(dec_cols.at[image], hidden, side, 2 * channels, half * channels)
            if tick == 0 and image == 0:
                for copy in loads[9:10] + loads[11:]:
                    copy.wait()
            conv_add(
                decoded, dec_pack, tick * images + image, dec_cols.at[image], wd, dec_tail, True, current, bd[...],
                side,
            )
            if tick < ticks - 1:

                @pl.when(me < sections - 1)
                def _():
                    dec_next(tick, image).start()

    for image in range(images):
        to_mirror(ticks - 1, image).wait_recv()
        keep_mirrored(ticks - 1, image)
    for tick in range(ticks):
        for image in range(images):
            to_mirror(tick, image).wait_send()
            if tick < ticks - 1:
                if sections > 2:

                    @pl.when(ahead)
                    def _():
                        enc_next(tick, image).wait_send()

                @pl.when(me < sections - 1)
                def _():
                    dec_next(tick, image).wait_send()


def hand_on(*refs):
    count = len(refs) // 2
    copies = []
    for source, target in zip(refs[:count], refs[count:-1]):
        half = source.shape[0] // 2
        for part in range(2):
            at = pl.ds(part * half, half)
            copies.append(pltpu.make_async_copy(source.at[at], target.at[at], refs[-1].at[len(copies)]))
    for copy in copies:
        copy.start()
    for copy in copies:
        copy.wait()


def shards(sections, enc_in, dec_in, fresh, skip_queue, enc_weight, enc_bias, enc_gain, enc_beta,
           dec_weight, dec_bias, dec_gain, dec_beta):
    images, side, _, channels = enc_in.shape
    ticks = skip_queue.shape[0] // images
    rows = side * side

    def flat(maps):
        return maps.reshape(maps.shape[0] * rows, channels)

    def taps(kernel):
        return kernel.reshape(3, 3 * channels, channels)

    operands = (
        flat(enc_in), flat(dec_in), flat(fresh), flat(skip_queue),
        taps(enc_weight), enc_bias, enc_gain, enc_beta,
        lax.transpose(dec_weight, (0, 1, 2, 4, 3)).reshape(9, channels, 2 * channels), dec_bias, dec_gain, dec_beta,
    )
    total = ticks * images * rows
    maps = jax.ShapeDtypeStruct((total, channels), BF16)
    narrow = channels % LANES
    wide = channels - narrow
    packed = pltpu.VMEM((ticks * images * rows * channels // wide, wide), BF16)
    spare = packed if sections > 2 else pltpu.VMEM((16, wide), BF16)
    held = [pltpu.VMEM(value.shape, value.dtype) for value in operands]
    held[8] = pltpu.VMEM((3, wide, 6 * channels), BF16)
    steps = ticks * images
    anywhere = pl.BlockSpec(memory_space=pl.ANY)
    outs = pl.pallas_call(
        functools.partial(relay, sections, ticks, images, side),
        out_shape=(pltpu.VMEM(maps.shape, maps.dtype),) * 3,
        in_specs=[anywhere] * len(operands),
        out_specs=[pl.BlockSpec(memory_space=pltpu.VMEM)] * 3,
        scratch_shapes=held
        + [
            packed,
            packed,
            packed,
            spare,
            packed,
            pltpu.VMEM((images, rows + 2 * side, 3 * channels), BF16),
            pltpu.VMEM((images, rows + 2 * side, 6 * channels), BF16),
            pltpu.VMEM((3 * channels, 3 * narrow), BF16),
            pltpu.VMEM((3 * narrow, 6 * channels), BF16),
            pltpu.SemaphoreType.DMA((len(operands) + 17,)),
        ]
        + [pltpu.SemaphoreType.DMA((steps,))] * 6,
        compiler_params=pltpu.CompilerParams(
            collective_id=0, has_side_effects=True, vmem_limit_bytes=56 * 1024 * 1024
        ),
        cost_estimate=pl.CostEstimate(
            flops=steps * rows * 2 * 27 * channels * channels, bytes_accessed=12 * 1024 * 1024, transcendentals=0
        ),
    )(*operands)
    outs = pl.pallas_call(
        hand_on,
        out_shape=(maps, maps, maps),
        in_specs=[anywhere] * 3,
        out_specs=[anywhere] * 3,
        scratch_shapes=[pltpu.SemaphoreType.DMA((6,))],
        compiler_params=pltpu.CompilerParams(vmem_limit_bytes=4 * 1024 * 1024),
    )(*outs)
    return tuple(out.reshape(ticks * images, side, side, channels) for out in outs)


def solution(mesh):
    maps = P(("dp", "section"), None, None, None)
    row = P("section", None)
    kernel = P("section", None, None, None, None)
    in_specs = (maps, maps, P("dp", None, None, None), maps, kernel, row, row, row, kernel, row, row, row)
    return jax.shard_map(
        functools.partial(shards, mesh.shape["section"]),
        mesh=mesh,
        in_specs=in_specs,
        out_specs=(maps, maps, maps),
        check_vma=False,
    )
```

```python
import functools

import jax
import jax.numpy as jnp
from jax import lax
from jax.experimental import pallas as pl
from jax.experimental.pallas import tpu as pltpu
from jax.sharding import PartitionSpec as P

GROUPS = 32
LANES = 256
F32 = jnp.float32
BF16 = jnp.bfloat16
MESH = pl.DeviceIdType.MESH


def membership(width, per_group):
    row = lax.broadcasted_iota(jnp.int32, (width, width), 0).astype(F32)
    column = lax.broadcasted_iota(jnp.int32, (width, width), 1).astype(F32)
    same = jnp.floor((row + 0.5) * (1.0 / per_group)) == jnp.floor((column + 0.5) * (1.0 / per_group))
    return jnp.where(same, 1.0, 0.0).astype(BF16)


def group_total(values, member):
    part = jnp.sum(values.reshape(values.shape[0] // 8, 8, values.shape[1]), axis=0)
    high = part.astype(BF16).astype(F32)
    rest = part - high
    middle = rest.astype(BF16).astype(F32)
    low = rest - middle
    pieces = jnp.concatenate([high, middle, low], axis=0).astype(BF16)
    return jnp.sum(jnp.dot(pieces, member, preferred_element_type=F32), axis=0, keepdims=True)


def prepare(values, member, per_group, gain, beta, buffer, side, pitch, offset):
    share = 1.0 / (values.shape[0] * per_group)
    centred = values - group_total(values, member) * share
    yield
    variance = group_total(centred * centred, member) * share
    yield
    half = centred * (lax.rsqrt(variance + 1e-05) * (0.5 * gain)) + 0.5 * beta
    hidden = half + half * jnp.tanh(half)
    rows, width = hidden.shape
    cell = lax.rem(lax.broadcasted_iota(jnp.int32, (rows, width), 0), side)
    buffer[side : side + rows, pitch + offset : pitch + offset + width] = hidden.astype(BF16)
    yield
    before = jnp.where(cell == 0, 0.0, pltpu.roll(hidden, 1, 0))
    buffer[side : side + rows, offset : offset + width] = before.astype(BF16)
    yield
    after = jnp.where(cell == side - 1, 0.0, pltpu.roll(hidden, rows - 1, 0))
    buffer[side : side + rows, 2 * pitch + offset : 2 * pitch + offset + width] = after.astype(BF16)


def weave(*works):
    works = list(works)
    while works:
        for work in tuple(works):
            try:
                next(work)
            except StopIteration:
                works.remove(work)


def product(left, right, flipped):
    return lax.dot_general(left, right, (((1,), (1 if flipped else 0,)), ((), ())), preferred_element_type=F32)


def pack(target, start, wide, tail):
    rows, narrow = tail.shape
    depth = rows * narrow // wide.shape[1]
    target[start : start + rows, :] = wide
    for part in range(rows // depth):
        target[start + rows : start + rows + depth, part * narrow : (part + 1) * narrow] = tail[
            part * depth : (part + 1) * depth, :
        ]


def unpack(source, start, rows, narrow):
    depth = rows * narrow // source.shape[1]
    tail = [
        source[start + rows : start + rows + depth, part * narrow : (part + 1) * narrow]
        for part in range(rows // depth)
    ]
    return source[start : start + rows, :], jnp.concatenate(tail, axis=0)


def conv_add(out, packed, step, buffer, weight, tail, flipped, source, bias, side):
    rows, width = source.shape
    start = step * rows
    wide = width // LANES * LANES
    narrow = width - wide
    total = source[:, :wide] + bias[:, :wide]
    for tap in range(3):
        total += product(
            buffer[tap * side : tap * side + rows, :], weight[tap] if flipped else weight[tap, :, :wide], flipped
        )
        yield
    main = total.astype(BF16)
    out[start : start + rows, :wide] = main
    ends = product(buffer[...], tail[...], flipped)
    yield
    total = source[:, wide:] + bias[:, wide:]
    for tap in range(3):
        total += ends[tap * side : tap * side + rows, tap * narrow : (tap + 1) * narrow]
    rest = total.astype(BF16)
    out[start : start + rows, wide:] = rest
    pack(packed, step * packed.shape[0] // (out.shape[0] // rows), main, rest)


def relay(sections, ticks, images, side, *refs):
    (enc_in, dec_in, fresh, queue, enc_w, enc_b, enc_g, enc_o, dec_w, dec_b, dec_g, dec_o) = refs[:12]
    (encoded, decoded, queued) = refs[12:15]
    (e0, d0, fr, sk, we, be, ge, oe, wd, bd, gd, od) = refs[15:27]
    (enc_pack, dec_pack, q_buf, e_buf, d_buf, enc_cols, dec_cols, enc_tail, dec_tail) = refs[27:36]
    (load_sem, q_send, q_recv, e_send, e_recv, d_send, d_recv) = refs[36:]
    me = lax.axis_index("section")
    mirror = sections - 1 - me
    rows = side * side
    channels = e0.shape[1]
    wide = channels // LANES * LANES
    narrow = channels - wide
    packed = rows * channels // wide

    barrier = pltpu.get_barrier_semaphore()
    pl.semaphore_signal(barrier, inc=1, device_id={"section": mirror}, device_id_type=MESH)
    if sections > 2:
        behind = jnp.logical_and(me > 0, me - 1 != mirror)
        ahead = jnp.logical_and(me < sections - 1, me + 1 != mirror)

        @pl.when(behind)
        def _():
            pl.semaphore_signal(barrier, inc=1, device_id={"section": me - 1}, device_id_type=MESH)

    loads = []
    moves = [
        (enc_in, e0), (enc_g, ge), (enc_o, oe), (enc_w, we), (enc_b, be), (dec_in, d0), (queue, sk),
        (dec_g, gd), (dec_o, od), (dec_b, bd), (fresh, fr),
    ]
    for tap in range(9):
        lanes = pl.ds(tap % 3 * 2 * channels, 2 * channels)
        source = dec_w.at[tap]
        moves.append((source.at[pl.ds(0, wide)], wd.at[tap // 3, :, lanes]))
        moves.append((source.at[pl.ds(wide, narrow)], dec_tail.at[pl.ds(tap // 3 * narrow, narrow), lanes]))
    for source, target in moves:
        copy = pltpu.make_async_copy(source, target, load_sem.at[len(loads)])
        loads.append(copy)
    for copy in loads[:5]:
        copy.start()

    def span(tick, image):
        return pl.ds((tick * images + image) * rows, rows)

    def bundle(tick, image):
        return pl.ds((tick * images + image) * packed, packed)

    def opened(source, tick, image):
        return unpack(source, (tick * images + image) * packed, rows, narrow)

    def joined(source, tick, image):
        return jnp.concatenate([part.astype(F32) for part in opened(source, tick, image)], axis=1)

    def keep_mirrored(tick, image):
        main, rest = opened(q_buf, tick, image)
        start = (tick * images + image) * rows
        queued[start : start + rows, :wide] = main
        queued[start : start + rows, wide:] = rest

    def to_mirror(tick, image):
        return pltpu.make_async_remote_copy(
            src_ref=enc_pack.at[bundle(tick, image)],
            dst_ref=q_buf.at[bundle(tick, image)],
            send_sem=q_send.at[tick * images + image],
            recv_sem=q_recv.at[tick * images + image],
            device_id={"section": mirror},
            device_id_type=MESH,
        )

    def to_next(source, target, send, recv, tick, image):
        return pltpu.make_async_remote_copy(
            src_ref=source.at[bundle(tick, image)],
            dst_ref=target.at[bundle(tick, image)],
            send_sem=send.at[tick * images + image],
            recv_sem=recv.at[tick * images + image],
            device_id={"section": lax.rem(me + 1, sections)},
            device_id_type=MESH,
        )

    enc_next = functools.partial(to_next, enc_pack, e_buf, e_send, e_recv)
    dec_next = functools.partial(to_next, dec_pack, d_buf, d_send, d_recv)

    def clear(columns):
        edge = jnp.zeros((images, side, columns.shape[2]), BF16)
        columns[:, :side, :] = edge
        columns[:, side + rows :, :] = edge

    def enc_source(tick, image):
        if tick == 0:
            return e0[image * rows : (image + 1) * rows, :].astype(F32)
        moved = joined(q_buf, tick - 1, image)
        if sections > 2:
            moved = jnp.where(me - 1 == mirror, moved, joined(e_buf, tick - 1, image))
        return jnp.where(me == 0, fr[span(tick - 1, image), :].astype(F32), moved)

    def dec_source(tick, image):
        if tick == 0:
            return d0[image * rows : (image + 1) * rows, :].astype(F32)
        return jnp.where(me == 0, joined(q_buf, tick - 1, image), joined(d_buf, tick - 1, image))

    def dec_skip(tick, image):
        skipped = sk[span(tick, image), :].astype(F32)
        return skipped if tick == 0 else jnp.where(me == 0, joined(q_buf, tick - 1, image), skipped)

    def arrive(is_enc, tick, image):
        if tick == 0:
            if image == 0 and not is_enc:
                for copy in loads[5:9]:
                    copy.wait()
            return
        if is_enc:
            if tick == 1 and image == 0:
                loads[10].wait()
            to_mirror(tick - 1, image).wait_recv()
            if sections > 2:

                @pl.when(behind)
                def _():
                    enc_next(tick - 1, image).wait_recv()

            return

        @pl.when(me > 0)
        def _():
            dec_next(tick - 1, image).wait_recv()

    def ready(is_enc, tick, image):
        if is_enc:
            if tick > 0:
                keep_mirrored(tick - 1, image)
            yield from prepare(
                enc_source(tick, image), enc_member, channels // GROUPS, ge[...], oe[...], enc_cols.at[image],
                side, channels, 0,
            )
            return
        parts = []
        for half, values in enumerate((dec_source(tick, image), dec_skip(tick, image))):
            lanes = slice(half * channels, (half + 1) * channels)
            parts.append(
                prepare(
                    values, dec_member, 2 * channels // GROUPS, gd[:, lanes], od[:, lanes], dec_cols.at[image],
                    side, 2 * channels, half * channels,
                )
            )
        while parts:
            for part in tuple(parts):
                try:
                    next(part)
                except StopIteration:
                    parts.remove(part)
            yield

    def convolve(is_enc, tick, image):
        step = tick * images + image
        if is_enc:
            return conv_add(
                encoded, enc_pack, step, enc_cols.at[image], we, enc_tail, False, enc_source(tick, image), be[...], side
            )
        return conv_add(
            decoded, dec_pack, step, dec_cols.at[image], wd, dec_tail, True, dec_source(tick, image), bd[...], side
        )

    def send(is_enc, tick, image):
        if is_enc:
            if tick == 0 and image == 0:
                pl.semaphore_wait(barrier, 1)
                if sections > 2:

                    @pl.when(ahead)
                    def _():
                        pl.semaphore_wait(barrier, 1)

            to_mirror(tick, image).start()
            if sections > 2 and tick < ticks - 1:

                @pl.when(ahead)
                def _():
                    enc_next(tick, image).start()

        elif tick < ticks - 1:

            @pl.when(me < sections - 1)
            def _():
                dec_next(tick, image).start()

    stages = [
        (is_enc, tick, image) for tick in range(ticks) for is_enc in (True, False) for image in range(images)
    ]
    enc_member = membership(channels, channels // GROUPS)
    clear(enc_cols)
    for copy in loads[:3]:
        copy.wait()
    weave(ready(*stages[0]))
    for copy in loads[3:5]:
        copy.wait()
    for copy in loads[5:]:
        copy.start()
    for tap in range(3):
        enc_tail[:, tap * narrow : (tap + 1) * narrow] = we[tap, :, wide:]
    dec_member = None
    for index, stage in enumerate(stages):
        following = stages[index + 1 : index + 2]
        for coming in following:
            arrive(*coming)
            if dec_member is None and not coming[0]:
                dec_member = membership(channels, 2 * channels // GROUPS)
                clear(dec_cols)
        if stage == (False, 0, 0):
            for copy in loads[9:10] + loads[11:]:
                copy.wait()
        weave(convolve(*stage), *[ready(*coming) for coming in following])
        send(*stage)

    for image in range(images):
        to_mirror(ticks - 1, image).wait_recv()
        keep_mirrored(ticks - 1, image)
    for tick in range(ticks):
        for image in range(images):
            to_mirror(tick, image).wait_send()
            if tick < ticks - 1:
                if sections > 2:

                    @pl.when(ahead)
                    def _():
                        enc_next(tick, image).wait_send()

                @pl.when(me < sections - 1)
                def _():
                    dec_next(tick, image).wait_send()


def hand_on(*refs):
    count = len(refs) // 2
    copies = []
    for source, target in zip(refs[:count], refs[count:-1]):
        half = source.shape[0] // 2
        for part in range(2):
            at = pl.ds(part * half, half)
            copies.append(pltpu.make_async_copy(source.at[at], target.at[at], refs[-1].at[len(copies)]))
    for copy in copies:
        copy.start()
    for copy in copies:
        copy.wait()


def shards(sections, enc_in, dec_in, fresh, skip_queue, enc_weight, enc_bias, enc_gain, enc_beta,
           dec_weight, dec_bias, dec_gain, dec_beta):
    images, side, _, channels = enc_in.shape
    ticks = skip_queue.shape[0] // images
    rows = side * side

    def flat(maps):
        return maps.reshape(maps.shape[0] * rows, channels)

    def taps(kernel):
        return kernel.reshape(3, 3 * channels, channels)

    operands = (
        flat(enc_in), flat(dec_in), flat(fresh), flat(skip_queue),
        taps(enc_weight), enc_bias, enc_gain, enc_beta,
        lax.transpose(dec_weight, (0, 1, 2, 4, 3)).reshape(9, channels, 2 * channels), dec_bias, dec_gain, dec_beta,
    )
    total = ticks * images * rows
    maps = jax.ShapeDtypeStruct((total, channels), BF16)
    narrow = channels % LANES
    wide = channels - narrow
    packed = pltpu.VMEM((ticks * images * rows * channels // wide, wide), BF16)
    spare = packed if sections > 2 else pltpu.VMEM((16, wide), BF16)
    held = [pltpu.VMEM(value.shape, value.dtype) for value in operands]
    held[8] = pltpu.VMEM((3, wide, 6 * channels), BF16)
    steps = ticks * images
    anywhere = pl.BlockSpec(memory_space=pl.ANY)
    outs = pl.pallas_call(
        functools.partial(relay, sections, ticks, images, side),
        out_shape=(pltpu.VMEM(maps.shape, maps.dtype),) * 3,
        in_specs=[anywhere] * len(operands),
        out_specs=[pl.BlockSpec(memory_space=pltpu.VMEM)] * 3,
        scratch_shapes=held
        + [
            packed,
            packed,
            packed,
            spare,
            packed,
            pltpu.VMEM((images, rows + 2 * side, 3 * channels), BF16),
            pltpu.VMEM((images, rows + 2 * side, 6 * channels), BF16),
            pltpu.VMEM((3 * channels, 3 * narrow), BF16),
            pltpu.VMEM((3 * narrow, 6 * channels), BF16),
            pltpu.SemaphoreType.DMA((len(operands) + 17,)),
        ]
        + [pltpu.SemaphoreType.DMA((steps,))] * 6,
        compiler_params=pltpu.CompilerParams(
            collective_id=0, has_side_effects=True, vmem_limit_bytes=56 * 1024 * 1024
        ),
        cost_estimate=pl.CostEstimate(
            flops=steps * rows * 2 * 27 * channels * channels, bytes_accessed=12 * 1024 * 1024, transcendentals=0
        ),
    )(*operands)
    outs = pl.pallas_call(
        hand_on,
        out_shape=(maps, maps, maps),
        in_specs=[anywhere] * 3,
        out_specs=[anywhere] * 3,
        scratch_shapes=[pltpu.SemaphoreType.DMA((6,))],
        compiler_params=pltpu.CompilerParams(vmem_limit_bytes=4 * 1024 * 1024),
    )(*outs)
    return tuple(out.reshape(ticks * images, side, side, channels) for out in outs)


def solution(mesh):
    maps = P(("dp", "section"), None, None, None)
    row = P("section", None)
    kernel = P("section", None, None, None, None)
    in_specs = (maps, maps, P("dp", None, None, None), maps, kernel, row, row, row, kernel, row, row, row)
    return jax.shard_map(
        functools.partial(shards, mesh.shape["section"]),
        mesh=mesh,
        in_specs=in_specs,
        out_specs=(maps, maps, maps),
        check_vma=False,
    )
```

```python
import functools

import jax
import jax.numpy as jnp
from jax import lax
from jax.experimental import pallas as pl
from jax.experimental.pallas import tpu as pltpu
from jax.sharding import PartitionSpec as P

GROUPS = 32
STRIPS = 2
LANES = 256
F32 = jnp.float32
BF16 = jnp.bfloat16
MESH = pl.DeviceIdType.MESH


def membership(width, per_group):
    row = lax.broadcasted_iota(jnp.int32, (width, width), 0).astype(F32)
    column = lax.broadcasted_iota(jnp.int32, (width, width), 1).astype(F32)
    same = jnp.floor((row + 0.5) * (1.0 / per_group)) == jnp.floor((column + 0.5) * (1.0 / per_group))
    return jnp.where(same, 1.0, 0.0).astype(BF16)


def group_total(values, member):
    part = jnp.sum(values.reshape(values.shape[0] // 8, 8, values.shape[1]), axis=0)
    high = part.astype(BF16).astype(F32)
    rest = part - high
    middle = rest.astype(BF16).astype(F32)
    low = rest - middle
    pieces = jnp.concatenate([high, middle, low], axis=0).astype(BF16)
    return jnp.sum(jnp.dot(pieces, member, preferred_element_type=F32), axis=0, keepdims=True)


def prepare(values, member, per_group, gain, beta, buffer, side, pitch, offset):
    share = 1.0 / (values.shape[0] * per_group)
    centred = values - group_total(values, member) * share
    yield
    variance = group_total(centred * centred, member) * share
    yield
    half = centred * (lax.rsqrt(variance + 1e-05) * (0.5 * gain)) + 0.5 * beta
    hidden = half + half * jnp.tanh(half)
    rows, width = hidden.shape
    cell = lax.rem(lax.broadcasted_iota(jnp.int32, (rows, width), 0), side)
    buffer[side : side + rows, pitch + offset : pitch + offset + width] = hidden.astype(BF16)
    yield
    before = jnp.where(cell == 0, 0.0, pltpu.roll(hidden, 1, 0))
    buffer[side : side + rows, offset : offset + width] = before.astype(BF16)
    yield
    after = jnp.where(cell == side - 1, 0.0, pltpu.roll(hidden, rows - 1, 0))
    buffer[side : side + rows, 2 * pitch + offset : 2 * pitch + offset + width] = after.astype(BF16)


def weave(*works):
    works = list(works)
    while works:
        for work in tuple(works):
            try:
                next(work)
            except StopIteration:
                works.remove(work)


def product(left, right, flipped):
    return lax.dot_general(left, right, (((1,), (1 if flipped else 0,)), ((), ())), preferred_element_type=F32)


def pack(target, start, wide, tail):
    rows, narrow = tail.shape
    depth = rows * narrow // wide.shape[1]
    target[start : start + rows, :] = wide
    for part in range(rows // depth):
        target[start + rows : start + rows + depth, part * narrow : (part + 1) * narrow] = tail[
            part * depth : (part + 1) * depth, :
        ]


def unpack(source, start, rows, narrow):
    depth = rows * narrow // source.shape[1]
    tail = [
        source[start + rows : start + rows + depth, part * narrow : (part + 1) * narrow]
        for part in range(rows // depth)
    ]
    return source[start : start + rows, :], jnp.concatenate(tail, axis=0)


def conv_add(out, packed, step, buffer, weight, tail, flipped, source, bias, side, strips):
    strip = source.shape[0] // STRIPS
    first, rows = strips[0] * strip, len(strips) * strip
    start = step * source.shape[0] + first
    block = packed.shape[0] * strip // out.shape[0]
    source = source[first : first + rows, :]
    width = source.shape[1]
    wide = width // LANES * LANES
    narrow = width - wide
    total = source[:, :wide] + bias[:, :wide]
    for tap in range(3):
        total += product(
            buffer[first + tap * side : first + tap * side + rows, :], weight[tap] if flipped else weight[tap, :, :wide], flipped
        )
        yield
    main = total.astype(BF16)
    out[start : start + rows, :wide] = main
    ends = product(buffer[first : first + rows + 2 * side, :], tail[...], flipped)
    yield
    total = source[:, wide:] + bias[:, wide:]
    for tap in range(3):
        total += ends[tap * side : tap * side + rows, tap * narrow : (tap + 1) * narrow]
    rest = total.astype(BF16)
    out[start : start + rows, wide:] = rest
    for place, part in enumerate(strips):
        lines = slice(place * strip, (place + 1) * strip)
        pack(packed, (step * STRIPS + part) * block, main[lines], rest[lines])


def relay(sections, ticks, images, side, *refs):
    (enc_in, dec_in, fresh, queue, enc_w, enc_b, enc_g, enc_o, dec_w, dec_b, dec_g, dec_o) = refs[:12]
    (encoded, decoded, queued) = refs[12:15]
    (e0, d0, fr, sk, we, be, ge, oe, wd, bd, gd, od) = refs[15:27]
    (enc_pack, dec_pack, q_buf, e_buf, d_buf, enc_cols, dec_cols, enc_tail, dec_tail) = refs[27:36]
    (load_sem, q_send, q_recv, e_send, e_recv, d_send, d_recv) = refs[36:]
    me = lax.axis_index("section")
    mirror = sections - 1 - me
    rows = side * side
    channels = e0.shape[1]
    wide = channels // LANES * LANES
    narrow = channels - wide
    packed = rows * channels // wide

    barrier = pltpu.get_barrier_semaphore()
    pl.semaphore_signal(barrier, inc=1, device_id={"section": mirror}, device_id_type=MESH)
    if sections > 2:
        behind = jnp.logical_and(me > 0, me - 1 != mirror)
        ahead = jnp.logical_and(me < sections - 1, me + 1 != mirror)

        @pl.when(behind)
        def _():
            pl.semaphore_signal(barrier, inc=1, device_id={"section": me - 1}, device_id_type=MESH)

    loads = []
    moves = [
        (enc_in, e0), (enc_g, ge), (enc_o, oe), (enc_w, we), (enc_b, be), (dec_in, d0), (queue, sk),
        (dec_g, gd), (dec_o, od), (dec_b, bd), (fresh, fr),
    ]
    for tap in range(9):
        lanes = pl.ds(tap % 3 * 2 * channels, 2 * channels)
        source = dec_w.at[tap]
        moves.append((source.at[pl.ds(0, wide)], wd.at[tap // 3, :, lanes]))
        moves.append((source.at[pl.ds(wide, narrow)], dec_tail.at[pl.ds(tap // 3 * narrow, narrow), lanes]))
    for source, target in moves:
        copy = pltpu.make_async_copy(source, target, load_sem.at[len(loads)])
        loads.append(copy)
    for copy in loads[:5]:
        copy.start()

    def span(tick, image):
        return pl.ds((tick * images + image) * rows, rows)

    def bundle(tick, image):
        return pl.ds((tick * images + image) * packed, packed)

    def opened(source, tick, image):
        start = (tick * images + image) * packed
        parts = [
            unpack(source, start + part * packed // STRIPS, rows // STRIPS, narrow) for part in range(STRIPS)
        ]
        return [jnp.concatenate(pieces, axis=0) for pieces in zip(*parts)]

    def joined(source, tick, image):
        return jnp.concatenate([part.astype(F32) for part in opened(source, tick, image)], axis=1)

    def keep_mirrored(tick, image):
        main, rest = opened(q_buf, tick, image)
        start = (tick * images + image) * rows
        queued[start : start + rows, :wide] = main
        queued[start : start + rows, wide:] = rest

    def to_mirror(tick, image):
        step = tick * images + image
        pieces = [(step, step * packed, packed)]
        if step == 0:
            block = packed // STRIPS
            pieces = [(part if part == 0 else ticks * images + part - 1, part * block, block) for part in range(STRIPS)]
        return [
            pltpu.make_async_remote_copy(
                src_ref=enc_pack.at[pl.ds(start, size)],
                dst_ref=q_buf.at[pl.ds(start, size)],
                send_sem=q_send.at[slot],
                recv_sem=q_recv.at[slot],
                device_id={"section": mirror},
                device_id_type=MESH,
            )
            for slot, start, size in pieces
        ]

    def to_next(source, target, send, recv, tick, image):
        return pltpu.make_async_remote_copy(
            src_ref=source.at[bundle(tick, image)],
            dst_ref=target.at[bundle(tick, image)],
            send_sem=send.at[tick * images + image],
            recv_sem=recv.at[tick * images + image],
            device_id={"section": lax.rem(me + 1, sections)},
            device_id_type=MESH,
        )

    enc_next = functools.partial(to_next, enc_pack, e_buf, e_send, e_recv)
    dec_next = functools.partial(to_next, dec_pack, d_buf, d_send, d_recv)

    def clear(columns):
        edge = jnp.zeros((images, side, columns.shape[2]), BF16)
        columns[:, :side, :] = edge
        columns[:, side + rows :, :] = edge

    def enc_source(tick, image):
        if tick == 0:
            return e0[image * rows : (image + 1) * rows, :].astype(F32)
        moved = joined(q_buf, tick - 1, image)
        if sections > 2:
            moved = jnp.where(me - 1 == mirror, moved, joined(e_buf, tick - 1, image))
        return jnp.where(me == 0, fr[span(tick - 1, image), :].astype(F32), moved)

    def dec_source(tick, image):
        if tick == 0:
            return d0[image * rows : (image + 1) * rows, :].astype(F32)
        return jnp.where(me == 0, joined(q_buf, tick - 1, image), joined(d_buf, tick - 1, image))

    def dec_skip(tick, image):
        skipped = sk[span(tick, image), :].astype(F32)
        return skipped if tick == 0 else jnp.where(me == 0, joined(q_buf, tick - 1, image), skipped)

    def arrive(is_enc, tick, image):
        if tick == 0:
            if image == 0 and not is_enc:
                for copy in loads[5:9]:
                    copy.wait()
            return
        if is_enc:
            if tick == 1 and image == 0:
                loads[10].wait()
            for copy in to_mirror(tick - 1, image):
                copy.wait_recv()
            if sections > 2:

                @pl.when(behind)
                def _():
                    enc_next(tick - 1, image).wait_recv()

            return

        @pl.when(me > 0)
        def _():
            dec_next(tick - 1, image).wait_recv()

    def ready(is_enc, tick, image):
        if is_enc:
            if tick > 0:
                keep_mirrored(tick - 1, image)
            yield from prepare(
                enc_source(tick, image), enc_member, channels // GROUPS, ge[...], oe[...], enc_cols.at[image],
                side, channels, 0,
            )
            return
        parts = []
        for half, values in enumerate((dec_source(tick, image), dec_skip(tick, image))):
            lanes = slice(half * channels, (half + 1) * channels)
            parts.append(
                prepare(
                    values, dec_member, 2 * channels // GROUPS, gd[:, lanes], od[:, lanes], dec_cols.at[image],
                    side, 2 * channels, half * channels,
                )
            )
        while parts:
            for part in tuple(parts):
                try:
                    next(part)
                except StopIteration:
                    parts.remove(part)
            yield

    def convolve(is_enc, tick, image, strips):
        step = tick * images + image
        if is_enc:
            return conv_add(
                encoded, enc_pack, step, enc_cols.at[image], we, enc_tail, False, enc_source(tick, image), be[...],
                side, strips,
            )
        return conv_add(
            decoded, dec_pack, step, dec_cols.at[image], wd, dec_tail, True, dec_source(tick, image), bd[...],
            side, strips,
        )

    def send(is_enc, tick, image):
        if is_enc:
            for copy in to_mirror(tick, image)[-1:]:
                copy.start()
            if sections > 2 and tick < ticks - 1:

                @pl.when(ahead)
                def _():
                    enc_next(tick, image).start()

        elif tick < ticks - 1:

            @pl.when(me < sections - 1)
            def _():
                dec_next(tick, image).start()

    stages = [
        (is_enc, tick, image) for tick in range(ticks) for is_enc in (True, False) for image in range(images)
    ]
    enc_member = membership(channels, channels // GROUPS)
    clear(enc_cols)
    for copy in loads[:3]:
        copy.wait()
    weave(ready(*stages[0]))
    for copy in loads[3:5]:
        copy.wait()
    for copy in loads[5:]:
        copy.start()
    for tap in range(3):
        enc_tail[:, tap * narrow : (tap + 1) * narrow] = we[tap, :, wide:]
    for part in range(STRIPS - 1):
        weave(convolve(*stages[0], range(part, part + 1)))
        if part == 0:
            pl.semaphore_wait(barrier, 1)
            if sections > 2:

                @pl.when(ahead)
                def _():
                    pl.semaphore_wait(barrier, 1)

        to_mirror(0, 0)[part].start()
    dec_member = None
    for index, stage in enumerate(stages):
        following = stages[index + 1 : index + 2]
        for coming in following:
            arrive(*coming)
            if dec_member is None and not coming[0]:
                dec_member = membership(channels, 2 * channels // GROUPS)
                clear(dec_cols)
        if stage == (False, 0, 0):
            for copy in loads[9:10] + loads[11:]:
                copy.wait()
        strips = range(STRIPS) if index else range(STRIPS - 1, STRIPS)
        weave(convolve(*stage, strips), *[ready(*coming) for coming in following])
        send(*stage)

    for image in range(images):
        for copy in to_mirror(ticks - 1, image):
            copy.wait_recv()
        keep_mirrored(ticks - 1, image)
    for tick in range(ticks):
        for image in range(images):
            for copy in to_mirror(tick, image):
                copy.wait_send()
            if tick < ticks - 1:
                if sections > 2:

                    @pl.when(ahead)
                    def _():
                        enc_next(tick, image).wait_send()

                @pl.when(me < sections - 1)
                def _():
                    dec_next(tick, image).wait_send()


def hand_on(*refs):
    count = len(refs) // 2
    copies = []
    for source, target in zip(refs[:count], refs[count:-1]):
        size = source.shape[0] // 4
        for part in range(4):
            at = pl.ds(part * size, size)
            copies.append(pltpu.make_async_copy(source.at[at], target.at[at], refs[-1].at[len(copies)]))
    for copy in copies:
        copy.start()
    for copy in copies:
        copy.wait()


def shards(sections, enc_in, dec_in, fresh, skip_queue, enc_weight, enc_bias, enc_gain, enc_beta,
           dec_weight, dec_bias, dec_gain, dec_beta):
    images, side, _, channels = enc_in.shape
    ticks = skip_queue.shape[0] // images
    rows = side * side

    def flat(maps):
        return maps.reshape(maps.shape[0] * rows, channels)

    def taps(kernel):
        return kernel.reshape(3, 3 * channels, channels)

    operands = (
        flat(enc_in), flat(dec_in), flat(fresh), flat(skip_queue),
        taps(enc_weight), enc_bias, enc_gain, enc_beta,
        lax.transpose(dec_weight, (0, 1, 2, 4, 3)).reshape(9, channels, 2 * channels), dec_bias, dec_gain, dec_beta,
    )
    total = ticks * images * rows
    maps = jax.ShapeDtypeStruct((total, channels), BF16)
    narrow = channels % LANES
    wide = channels - narrow
    packed = pltpu.VMEM((ticks * images * rows * channels // wide, wide), BF16)
    spare = packed if sections > 2 else pltpu.VMEM((16, wide), BF16)
    held = [pltpu.VMEM(value.shape, value.dtype) for value in operands]
    held[8] = pltpu.VMEM((3, wide, 6 * channels), BF16)
    steps = ticks * images
    anywhere = pl.BlockSpec(memory_space=pl.ANY)
    outs = pl.pallas_call(
        functools.partial(relay, sections, ticks, images, side),
        out_shape=(pltpu.VMEM(maps.shape, maps.dtype),) * 3,
        in_specs=[anywhere] * len(operands),
        out_specs=[pl.BlockSpec(memory_space=pltpu.VMEM)] * 3,
        scratch_shapes=held
        + [
            packed,
            packed,
            packed,
            spare,
            packed,
            pltpu.VMEM((images, rows + 2 * side, 3 * channels), BF16),
            pltpu.VMEM((images, rows + 2 * side, 6 * channels), BF16),
            pltpu.VMEM((3 * channels, 3 * narrow), BF16),
            pltpu.VMEM((3 * narrow, 6 * channels), BF16),
            pltpu.SemaphoreType.DMA((len(operands) + 17,)),
        ]
        + [pltpu.SemaphoreType.DMA((steps + STRIPS - 1,))] * 6,
        compiler_params=pltpu.CompilerParams(
            collective_id=0, has_side_effects=True, vmem_limit_bytes=56 * 1024 * 1024
        ),
        cost_estimate=pl.CostEstimate(
            flops=steps * rows * 2 * 27 * channels * channels, bytes_accessed=12 * 1024 * 1024, transcendentals=0
        ),
    )(*operands)
    outs = pl.pallas_call(
        hand_on,
        out_shape=(maps, maps, maps),
        in_specs=[anywhere] * 3,
        out_specs=[anywhere] * 3,
        scratch_shapes=[pltpu.SemaphoreType.DMA((12,))],
        compiler_params=pltpu.CompilerParams(vmem_limit_bytes=4 * 1024 * 1024),
    )(*outs)
    return tuple(out.reshape(ticks * images, side, side, channels) for out in outs)


def solution(mesh):
    maps = P(("dp", "section"), None, None, None)
    row = P("section", None)
    kernel = P("section", None, None, None, None)
    in_specs = (maps, maps, P("dp", None, None, None), maps, kernel, row, row, row, kernel, row, row, row)
    return jax.shard_map(
        functools.partial(shards, mesh.shape["section"]),
        mesh=mesh,
        in_specs=in_specs,
        out_specs=(maps, maps, maps),
        check_vma=False,
    )
```
